1024 devices in a mesh: row: 64 (over z, x_lo, core), col: 16 (over y, x_hi).
Axes of the slice: x: 4 (x_hi: 2, x_lo: 2; x = x_hi * 2 + x_lo), y: 8, z: 16, core: 2. Of those that a mesh axis runs over, the one named last changes fastest.
Arguments:
- vectors: bfloat16 [8, 131072], P(None, ('row', 'col')), may hold values from -6 to 6
- tiles: bfloat16 [64, 16, 32, 128, 128], P('row', 'col'), may hold values from -0.125 to 0.125
- tile_rows: int32 [64, 16, 32], P('row', 'col'), may hold values from 0 to 15, as said below
- tile_cols: int32 [64, 16, 32], P('row', 'col'), may hold values from 0 to 63, as said below
- tile_live: int32 [64, 16, 32], P('row', 'col'), may hold values 0 or 1
Outputs:
- image: float32 [8, 131072], P(None, ('row', 'col'))
The draws below stay inside these ranges and needn't reach their ends.
Inputs may be any that keep to these rules, and one draw needn't show every extreme that they name: `tile_rows`: at least one slot of one device has the largest tile row. On grid row r, tile_cols is at most r.
All inputs are finite; a program needn't handle non-finite values. No bound on the sum of `tile_live` on one device may be relied on, other than what follows from the above.
Results may differ from the reference program's by a relative error of at most 0.0003.
Values may be sent and summed in bfloat16 or wider, within the bound.
No kernel may reach another device: no remote copies, remote signals or barrier semaphores. Data moves between devices by JAX's collectives and lax.ppermute only.
A program may use at most 32 MiB of HBM per device.

```python
import jax
import jax.numpy as jnp
from jax import lax

NVEC = 8
TILE = 128
STATES_DEV = 128
TILES_DEV = 32
STATES = 131072
N_ROW = 64
N_COL = 16


def draw_tile_rows(key, part):
    key = jax.random.fold_in(key, 11)
    per_seg = STATES_DEV // 128
    shape = (N_ROW, N_COL, TILES_DEV)
    drawn = jax.random.randint(key, shape, 0, N_COL * per_seg)
    first = (lax.broadcasted_iota(jnp.int32, shape, 0) == 0) & (lax.broadcasted_iota(jnp.int32, shape, 1) == 0) & (lax.broadcasted_iota(jnp.int32, shape, 2) == 0)
    return jnp.where(first, N_COL * per_seg - 1, drawn).astype(jnp.int32)


def draw_tile_cols(key, part):
    key = jax.random.fold_in(key, 23)
    per_seg = STATES_DEV // 128
    shape = (N_ROW, N_COL, TILES_DEV)
    grid_row = lax.broadcasted_iota(jnp.int32, shape, 0)
    drawn = jax.random.randint(key, shape, 0, (grid_row + 1) * per_seg)
    last = (grid_row == N_ROW - 1) & (lax.broadcasted_iota(jnp.int32, shape, 1) == 0) & (lax.broadcasted_iota(jnp.int32, shape, 2) == 0)
    return jnp.where(last, N_ROW * per_seg - 1, drawn).astype(jnp.int32)


def place_ends(entries, rng, low, top_value):
    longest = entries.shape.index(max(entries.shape))
    spots = []
    for shift in (0, 1):
        where = [jax.random.randint(jax.random.fold_in(rng, axis), (), 0, length) for axis, length in enumerate(entries.shape)]
        where[longest] = (where[longest] + shift) % entries.shape[longest]
        spots.append(tuple(where))
    return entries.at[spots[0]].set(low).at[spots[1]].set(top_value)


def block_scale(own_key, extent, split, least, top_value):
    def one(axis_at, parts):
        steps = jax.random.uniform(jax.random.fold_in(jax.random.fold_in(own_key, 6), axis_at), (parts,), jnp.float32, least / len(split), top_value / len(split))
        return jnp.repeat(jnp.exp(steps), extent[axis_at] // parts).reshape((-1,) + (1,) * (len(extent) - axis_at - 1))

    loudness = one(*split[0])
    for cut in split[1:]:
        loudness = loudness * one(*cut)
    return loudness


def scatter_about(key, shape, width, limit, shards=(), kind=jnp.bfloat16):
    level = block_scale(key, shape, shards, -0.22, 0.18) if shards else 1.0
    values = jax.random.normal(key, shape, jnp.float32) * width * level
    return jnp.minimum(jnp.maximum(values, -limit), limit).astype(kind)


def setup_inputs(seed: int = 0) -> dict:
    streams_of = jax.random.split(jax.random.key(seed), 6)
    return {
        "vectors": scatter_about(streams_of[0], (NVEC, STATES), 1.0, 6.0, ((1, 1024),)),
        "tiles": scatter_about(streams_of[1], (N_ROW, N_COL, TILES_DEV, TILE, TILE), 2048 ** -0.5, 0.125, ((0, 64), (1, 16))),
        "tile_rows": draw_tile_rows(jax.random.fold_in(streams_of[5], 71), 0),
        "tile_cols": draw_tile_cols(jax.random.fold_in(streams_of[5], 71), 0),
        "tile_live": place_ends((jax.random.randint(streams_of[4], (N_ROW, N_COL, TILES_DEV), 0, 4) < 3).astype(jnp.int32), jax.random.fold_in(streams_of[4], 1), 0, 1),
    }


def reference(vectors, tiles, tile_rows, tile_cols, tile_live):
    nvec = vectors.shape[0]
    per_seg = STATES_DEV // TILE
    total_tiles = N_ROW * N_COL * per_seg
    blocks_x = vectors.reshape(nvec, total_tiles, TILE)
    shape = (N_ROW, N_COL, TILES_DEV)
    grid_row = lax.broadcasted_iota(jnp.int32, shape, 0)
    grid_col = lax.broadcasted_iota(jnp.int32, shape, 1)
    grow = grid_row * N_COL * per_seg + tile_rows
    gcol = ((tile_cols // per_seg) * N_COL + grid_col) * per_seg + tile_cols % per_seg
    keep = tile_live == 1
    direct_weight = (keep & (grow >= gcol)).astype(jnp.float32)
    mirror_weight = (keep & (grow > gcol)).astype(jnp.float32)

    def step(acc, items):
        block, grs, gcs, dws, mws = items
        mats = block.reshape(-1, TILE, TILE).astype(jnp.float32)
        grs = grs.reshape(-1).astype(jnp.int32)
        gcs = gcs.reshape(-1).astype(jnp.int32)
        dws = dws.reshape(-1)
        mws = mws.reshape(-1)
        picked_cols = blocks_x[:, gcs, :].astype(jnp.float32)
        picked_rows = blocks_x[:, grs, :].astype(jnp.float32)
        direct = jnp.einsum('vmj,mij->vmi', picked_cols, mats, precision=lax.Precision.HIGHEST) * dws[None, :, None]
        mirror = jnp.einsum('vmi,mij->vmj', picked_rows, mats, precision=lax.Precision.HIGHEST) * mws[None, :, None]
        acc = acc.at[:, grs, :].add(direct)
        acc = acc.at[:, gcs, :].add(mirror)
        return acc, None

    start = jnp.zeros((nvec, total_tiles, TILE), jnp.float32)
    acc, unused = lax.scan(step, start, (tiles, grow, gcol, direct_weight, mirror_weight))
    return acc.reshape(nvec, total_tiles * TILE)
```

```python
import jax
import jax.numpy as jnp
from jax import lax
from jax.sharding import PartitionSpec as P


def exchange(parts, axis):
    return lax.all_to_all(parts, axis, 0, 0, tiled=True)


def body(vectors, tiles, tile_rows, tile_cols, tile_live):
    nvec, seg = vectors.shape
    n_row = lax.axis_size("row")
    n_col = lax.axis_size("col")
    my_row = lax.axis_index("row")
    my_col = lax.axis_index("col")
    blocks = tiles.reshape(-1, 128, 128)
    rows_local = tile_rows.reshape(-1)
    cols_local = tile_cols.reshape(-1)
    grow = my_row * n_col + rows_local
    gcol = cols_local * n_col + my_col
    keep = tile_live.reshape(-1) == 1
    direct_weight = (keep & (grow >= gcol)).astype(jnp.float32)
    mirror_weight = (keep & (grow > gcol)).astype(jnp.float32)

    row_set = exchange(jnp.broadcast_to(vectors[None], (n_col, nvec, seg)), "col")
    column_set = exchange(jnp.broadcast_to(vectors[None], (n_row, nvec, seg)), "row")

    picked = row_set[rows_local]
    product = jnp.einsum("kvi,kij->kvj", picked, blocks, preferred_element_type=jnp.float32)
    targets = lax.broadcasted_iota(jnp.int32, (n_row, 1), 0)
    placing = (cols_local[None, :] == targets).astype(jnp.float32) * mirror_weight[None, :]
    mirrored = exchange(jnp.einsum("rk,kvj->rvj", placing, product, precision=lax.Precision.HIGHEST), "row")

    picked = column_set[cols_local]
    product = jnp.einsum("kvj,kij->kvi", picked, blocks, preferred_element_type=jnp.float32)
    targets = lax.broadcasted_iota(jnp.int32, (n_col, 1), 0)
    placing = (rows_local[None, :] == targets).astype(jnp.float32) * direct_weight[None, :]
    straight = exchange(jnp.einsum("rk,kvi->rvi", placing, product, precision=lax.Precision.HIGHEST), "col")
    return jnp.sum(straight, axis=0) + jnp.sum(mirrored, axis=0)


def solution(mesh):
    return jax.shard_map(
        body,
        mesh=mesh,
        in_specs=(
            P(None, ("row", "col")),
            P("row", "col", None, None, None),
            P("row", "col", None),
            P("row", "col", None),
            P("row", "col", None),
        ),
        out_specs=P(None, ("row", "col")),
        check_vma=False,
    )
```

```python
import jax
import jax.numpy as jnp
from jax import lax
from jax.experimental import pallas as pl
from jax.experimental.pallas import tpu as pltpu
from jax.sharding import PartitionSpec as P

SMEM = pl.BlockSpec(memory_space=pltpu.SMEM)
VMEM = pl.BlockSpec(memory_space=pltpu.VMEM)


def exchange(parts, axis):
    return lax.all_to_all(parts, axis, 0, 0, tiled=True)


def mirror_kernel(slots, place, vec, row_set, tiles, parts):
    my_row = place[0]
    own = vec[...].astype(jnp.float32)
    for r in range(parts.shape[0]):
        parts[r] = jnp.where(r > my_row, own, 0.0)
    for k in range(tiles.shape[0]):
        product = jnp.dot(row_set[slots[0, k]], tiles[k], preferred_element_type=jnp.float32)
        weight = slots[3, k].astype(jnp.float32)
        parts[slots[1, k]] += product * weight


def direct_kernel(slots, place, vec, arrived, tiles, parts):
    my_row = place[0]
    parts[...] = jnp.zeros_like(parts)
    for k in range(tiles.shape[0]):
        source = slots[1, k]
        values = jnp.where(source == my_row, vec[...], arrived[source].astype(jnp.bfloat16))
        product = lax.dot_general(
            values, tiles[k], (((1,), (1,)), ((), ())), preferred_element_type=jnp.float32
        )
        weight = slots[2, k].astype(jnp.float32)
        parts[slots[0, k]] += product * weight


def body(vectors, tiles, tile_rows, tile_cols, tile_live):
    nvec, seg = vectors.shape
    n_row = lax.axis_size("row")
    n_col = lax.axis_size("col")
    my_row = lax.axis_index("row")
    my_col = lax.axis_index("col")
    blocks = tiles.reshape(-1, 128, 128)
    rows_local = tile_rows.reshape(-1)
    cols_local = tile_cols.reshape(-1)
    grow = my_row * n_col + rows_local
    gcol = cols_local * n_col + my_col
    keep = tile_live.reshape(-1) == 1
    direct_weight = (keep & (grow >= gcol)).astype(jnp.int32)
    mirror_weight = (keep & (grow > gcol)).astype(jnp.int32)
    slots = jnp.stack([rows_local, cols_local, direct_weight, mirror_weight])
    place = my_row.reshape(1)

    row_set = exchange(jnp.broadcast_to(vectors[None], (n_col, nvec, seg)), "col")
    outgoing = pl.pallas_call(
        mirror_kernel,
        out_shape=jax.ShapeDtypeStruct((n_row, nvec, seg), jnp.float32),
        in_specs=[SMEM, SMEM, VMEM, VMEM, VMEM],
        out_specs=VMEM,
        name="mirror",
        compiler_params=pltpu.CompilerParams(vmem_limit_bytes=4 << 20),
    )(slots, place, vectors, row_set, blocks)
    arrived = exchange(outgoing, "row")
    direct = pl.pallas_call(
        direct_kernel,
        out_shape=jax.ShapeDtypeStruct((n_col, nvec, seg), jnp.float32),
        in_specs=[SMEM, SMEM, VMEM, VMEM, VMEM],
        out_specs=VMEM,
        name="direct",
        compiler_params=pltpu.CompilerParams(vmem_limit_bytes=4 << 20),
    )(slots, place, vectors, arrived, blocks)
    straight = exchange(direct, "col")
    senders = lax.broadcasted_iota(jnp.int32, (n_row, 1, 1), 0)
    mirrored = jnp.sum(jnp.where(senders >= my_row, arrived, 0.0), axis=0)
    return mirrored + jnp.sum(straight, axis=0)


def solution(mesh):
    return jax.shard_map(
        body,
        mesh=mesh,
        in_specs=(
            P(None, ("row", "col")),
            P("row", "col", None, None, None),
            P("row", "col", None),
            P("row", "col", None),
            P("row", "col", None),
        ),
        out_specs=P(None, ("row", "col")),
        check_vma=False,
    )
```

```python
import jax
import jax.numpy as jnp
from jax import lax
from jax.experimental import pallas as pl
from jax.experimental.pallas import tpu as pltpu
from jax.sharding import PartitionSpec as P

SMEM = pl.BlockSpec(memory_space=pltpu.SMEM)
VMEM = pl.BlockSpec(memory_space=pltpu.VMEM)


def exchange(parts, axis):
    return lax.all_to_all(parts, axis, 0, 0, tiled=True)


def mirror_kernel(n_col, rows, cols, vec, row_set, tiles, parts):
    my_row, my_col = lax.axis_index("row"), lax.axis_index("col")
    own = vec[...].astype(jnp.float32)
    for r in range(parts.shape[0]):
        parts[r] = jnp.where(r > my_row, own, 0.0)
    for k in range(tiles.shape[0]):
        product = jnp.dot(row_set[rows[0, 0, k]], tiles[k], preferred_element_type=jnp.float32)
        below = my_row * n_col + rows[0, 0, k] > cols[0, 0, k] * n_col + my_col
        weight = jnp.where(below, 1.0, 0.0)
        parts[cols[0, 0, k]] += product * weight


def direct_kernel(n_col, rows, cols, vec, arrived, tiles, parts, mirrored):
    my_row, my_col = lax.axis_index("row"), lax.axis_index("col")
    total = jnp.zeros(mirrored.shape, jnp.float32)
    for r in range(arrived.shape[0]):
        total += jnp.where(r >= my_row, arrived[r], 0.0)
    mirrored[...] = total
    parts[...] = jnp.zeros_like(parts)
    for k in range(tiles.shape[0]):
        source = cols[0, 0, k]
        values = jnp.where(source == my_row, vec[...], arrived[source].astype(jnp.bfloat16))
        product = lax.dot_general(
            values, tiles[k], (((1,), (1,)), ((), ())), preferred_element_type=jnp.float32
        )
        below = my_row * n_col + rows[0, 0, k] >= source * n_col + my_col
        weight = jnp.where(below, 1.0, 0.0)
        parts[rows[0, 0, k]] += product * weight


def body(vectors, tiles, tile_rows, tile_cols, tile_live):
    nvec, seg = vectors.shape
    n_row = lax.axis_size("row")
    n_col = lax.axis_size("col")
    live = (tile_live.reshape(-1, 1, 1) == 1).astype(tiles.dtype)
    blocks = tiles.reshape(-1, 128, 128) * live
    params = pltpu.CompilerParams(vmem_limit_bytes=4 << 20)

    row_set = exchange(jnp.broadcast_to(vectors[None], (n_col, nvec, seg)), "col")
    outgoing = pl.pallas_call(
        lambda *refs: mirror_kernel(n_col, *refs),
        out_shape=jax.ShapeDtypeStruct((n_row, nvec, seg), jnp.float32),
        in_specs=[SMEM] * 2 + [VMEM] * 3,
        out_specs=VMEM,
        compiler_params=params,
        name="mirror",
    )(tile_rows, tile_cols, vectors, row_set, blocks)
    arrived = exchange(outgoing, "row")
    direct, mirrored = pl.pallas_call(
        lambda *refs: direct_kernel(n_col, *refs),
        out_shape=[
            jax.ShapeDtypeStruct((n_col, nvec, seg), jnp.float32),
            jax.ShapeDtypeStruct((nvec, seg), jnp.float32),
        ],
        in_specs=[SMEM] * 2 + [VMEM] * 3,
        out_specs=[VMEM, VMEM],
        compiler_params=params,
        name="direct",
    )(tile_rows, tile_cols, vectors, arrived, blocks)
    straight = exchange(direct, "col")
    return mirrored + jnp.sum(straight, axis=0)


def solution(mesh):
    return jax.shard_map(
        body,
        mesh=mesh,
        in_specs=(
            P(None, ("row", "col")),
            P("row", "col", None, None, None),
            P("row", "col", None),
            P("row", "col", None),
            P("row", "col", None),
        ),
        out_specs=P(None, ("row", "col")),
        check_vma=False,
    )
```

```python
import jax
import jax.numpy as jnp
from jax import lax
from jax.experimental import pallas as pl
from jax.experimental.pallas import tpu as pltpu
from jax.sharding import PartitionSpec as P

SMEM = pl.BlockSpec(memory_space=pltpu.SMEM)
VMEM = pl.BlockSpec(memory_space=pltpu.VMEM)


def exchange(parts, axis, order=None):
    groups = None if order is None else [order]
    return lax.all_to_all(parts, axis, 0, 0, tiled=True, axis_index_groups=groups)


def mirror_kernel(n_col, rows, cols, vec, row_set, tiles, parts):
    my_row, my_col = lax.axis_index("row"), lax.axis_index("col")
    own = vec[...].astype(jnp.float32)
    last = parts.shape[0] - 1
    for r in range(parts.shape[0]):
        parts[last - r] = jnp.where(r > my_row, own, 0.0)
    for k in range(tiles.shape[0]):
        product = jnp.dot(row_set[rows[0, 0, k]], tiles[k], preferred_element_type=jnp.float32)
        below = my_row * n_col + rows[0, 0, k] > cols[0, 0, k] * n_col + my_col
        weight = jnp.where(below, 1.0, 0.0)
        parts[last - cols[0, 0, k]] += product * weight


def direct_kernel(n_col, rows, cols, vec, arrived, tiles, parts, mirrored):
    my_row, my_col = lax.axis_index("row"), lax.axis_index("col")
    last = arrived.shape[0] - 1
    total = jnp.zeros(mirrored.shape, jnp.float32)
    for r in range(arrived.shape[0]):
        total += jnp.where(r >= my_row, arrived[last - r], 0.0)
    mirrored[...] = total
    parts[...] = jnp.zeros_like(parts)
    for k in range(tiles.shape[0]):
        source = cols[0, 0, k]
        values = jnp.where(source == my_row, vec[...], arrived[last - source].astype(jnp.bfloat16))
        product = lax.dot_general(
            values, tiles[k], (((1,), (1,)), ((), ())), preferred_element_type=jnp.float32
        )
        below = my_row * n_col + rows[0, 0, k] >= source * n_col + my_col
        weight = jnp.where(below, 1.0, 0.0)
        parts[rows[0, 0, k]] += product * weight


def body(vectors, tiles, tile_rows, tile_cols, tile_live):
    nvec, seg = vectors.shape
    n_row = lax.axis_size("row")
    n_col = lax.axis_size("col")
    live = (tile_live.reshape(-1, 1, 1) == 1).astype(tiles.dtype)
    blocks = tiles.reshape(-1, 128, 128) * live
    params = pltpu.CompilerParams(vmem_limit_bytes=4 << 20)

    row_set = exchange(jnp.broadcast_to(vectors[None], (n_col, nvec, seg)), "col")
    outgoing = pl.pallas_call(
        lambda *refs: mirror_kernel(n_col, *refs),
        out_shape=jax.ShapeDtypeStruct((n_row, nvec, seg), jnp.float32),
        in_specs=[SMEM] * 2 + [VMEM] * 3,
        out_specs=VMEM,
        compiler_params=params,
        name="mirror",
    )(tile_rows, tile_cols, vectors, row_set, blocks)
    arrived = exchange(outgoing, "row", list(range(n_row))[::-1])
    direct, mirrored = pl.pallas_call(
        lambda *refs: direct_kernel(n_col, *refs),
        out_shape=[
            jax.ShapeDtypeStruct((n_col, nvec, seg), jnp.float32),
            jax.ShapeDtypeStruct((nvec, seg), jnp.float32),
        ],
        in_specs=[SMEM] * 2 + [VMEM] * 3,
        out_specs=[VMEM, VMEM],
        compiler_params=params,
        name="direct",
    )(tile_rows, tile_cols, vectors, arrived, blocks)
    straight = exchange(direct, "col")
    return mirrored + jnp.sum(straight, axis=0)


def solution(mesh):
    return jax.shard_map(
        body,
        mesh=mesh,
        in_specs=(
            P(None, ("row", "col")),
            P("row", "col", None, None, None),
            P("row", "col", None),
            P("row", "col", None),
            P("row", "col", None),
        ),
        out_specs=P(None, ("row", "col")),
        check_vma=False,
    )
```

```python
import jax
import jax.numpy as jnp
from jax import lax
from jax.experimental import pallas as pl
from jax.experimental.pallas import tpu as pltpu
from jax.sharding import PartitionSpec as P

SMEM = pl.BlockSpec(memory_space=pltpu.SMEM)
VMEM = pl.BlockSpec(memory_space=pltpu.VMEM)


def row_sequence(n):
    planes = n // 4
    ring = [p + h for p in range(planes // 2) for h in (0, planes // 2)]
    return [4 * z + q for z in ring for q in range(4)]


def col_sequence(n):
    return [2 * y + x for p in range(n // 4) for y in (p, p + n // 4) for x in range(2)]


def exchange(parts, axis, order):
    return lax.all_to_all(parts, axis, 0, 0, tiled=True, axis_index_groups=[order])


def mirror_kernel(n_col, order, rows, cols, spot, seat, vec, row_set, tiles, parts):
    my_row, my_col = lax.axis_index("row"), lax.axis_index("col")
    own = vec[...].astype(jnp.float32)
    for at, r in enumerate(order):
        parts[at] = jnp.where(r > my_row, own, 0.0)
    for k in range(tiles.shape[0]):
        product = jnp.dot(row_set[seat[rows[0, 0, k]]], tiles[k], preferred_element_type=jnp.float32)
        below = my_row * n_col + rows[0, 0, k] > cols[0, 0, k] * n_col + my_col
        weight = jnp.where(below, 1.0, 0.0)
        parts[spot[cols[0, 0, k]]] += product * weight


def direct_kernel(n_col, order, rows, cols, spot, seat, vec, arrived, tiles, parts, mirrored):
    my_row, my_col = lax.axis_index("row"), lax.axis_index("col")
    total = jnp.zeros(mirrored.shape, jnp.float32)
    for at, r in enumerate(order):
        total += jnp.where(r >= my_row, arrived[at], 0.0)
    mirrored[...] = total
    parts[...] = jnp.zeros_like(parts)
    for k in range(tiles.shape[0]):
        source = cols[0, 0, k]
        values = jnp.where(source == my_row, vec[...], arrived[spot[source]].astype(jnp.bfloat16))
        product = lax.dot_general(
            values, tiles[k], (((1,), (1,)), ((), ())), preferred_element_type=jnp.float32
        )
        below = my_row * n_col + rows[0, 0, k] >= source * n_col + my_col
        weight = jnp.where(below, 1.0, 0.0)
        parts[seat[rows[0, 0, k]]] += product * weight


def body(vectors, tiles, tile_rows, tile_cols, tile_live):
    nvec, seg = vectors.shape
    n_row = lax.axis_size("row")
    n_col = lax.axis_size("col")
    row_order = row_sequence(n_row)
    row_spot = jnp.array([row_order.index(r) for r in range(n_row)], jnp.int32)
    col_order = col_sequence(n_col)
    col_spot = jnp.array([col_order.index(c) for c in range(n_col)], jnp.int32)
    live = (tile_live.reshape(-1, 1, 1) == 1).astype(tiles.dtype)
    blocks = tiles.reshape(-1, 128, 128) * live
    params = pltpu.CompilerParams(vmem_limit_bytes=4 << 20)

    row_set = exchange(jnp.broadcast_to(vectors[None], (n_col, nvec, seg)), "col", col_order)
    outgoing = pl.pallas_call(
        lambda *refs: mirror_kernel(n_col, row_order, *refs),
        out_shape=jax.ShapeDtypeStruct((n_row, nvec, seg), jnp.float32),
        in_specs=[SMEM] * 4 + [VMEM] * 3,
        out_specs=VMEM,
        compiler_params=params,
        name="mirror",
    )(tile_rows, tile_cols, row_spot, col_spot, vectors, row_set, blocks)
    arrived = exchange(outgoing, "row", row_order)
    direct, mirrored = pl.pallas_call(
        lambda *refs: direct_kernel(n_col, row_order, *refs),
        out_shape=[
            jax.ShapeDtypeStruct((n_col, nvec, seg), jnp.float32),
            jax.ShapeDtypeStruct((nvec, seg), jnp.float32),
        ],
        in_specs=[SMEM] * 4 + [VMEM] * 3,
        out_specs=[VMEM, VMEM],
        compiler_params=params,
        name="direct",
    )(tile_rows, tile_cols, row_spot, col_spot, vectors, arrived, blocks)
    straight = exchange(direct, "col", col_order)
    return mirrored + jnp.sum(straight, axis=0)


def solution(mesh):
    return jax.shard_map(
        body,
        mesh=mesh,
        in_specs=(
            P(None, ("row", "col")),
            P("row", "col", None, None, None),
            P("row", "col", None),
            P("row", "col", None),
            P("row", "col", None),
        ),
        out_specs=P(None, ("row", "col")),
        check_vma=False,
    )
```

```python
import jax
import jax.numpy as jnp
from jax import lax
from jax.experimental import pallas as pl
from jax.experimental.pallas import tpu as pltpu
from jax.sharding import PartitionSpec as P

SMEM = pl.BlockSpec(memory_space=pltpu.SMEM)
VMEM = pl.BlockSpec(memory_space=pltpu.VMEM)


def exchange(parts, axes, groups):
    return lax.all_to_all(parts, axes, 0, 0, tiled=True, axis_index_groups=groups)


def mirror_kernel(n_col, spots, lists, other_lists, row_sets, tiles, other_tiles, parts, sums):
    my_row, my_col = lax.axis_index("row"), lax.axis_index("col")
    pair, side = my_row // 2, my_row % 2
    pairs = parts.shape[0]
    sums[...] = jnp.zeros_like(sums)
    for k in range(tiles.shape[0]):
        for who, codes, blocks in ((side, lists, tiles), (1 - side, other_lists, other_tiles)):
            row, col = codes[0, k], codes[1, k]
            values = row_sets[who * n_col + row]
            product = jnp.dot(values, blocks[k], preferred_element_type=jnp.float32)
            below = (2 * pair + who) * n_col + row > col * n_col + my_col
            weight = jnp.where(below & (col % 2 == side) & (codes[2, k] == 1), 1.0, 0.0)
            sums[col // 2] += product * weight
    first, second = row_sets[my_col], row_sets[n_col + my_col]
    for p in range(pairs):
        high = sums[p].astype(jnp.bfloat16)
        low = (sums[p] - high.astype(jnp.float32)).astype(jnp.bfloat16)
        parts[spots[p], 0] = jnp.where(p > pair, first, high)
        parts[spots[p], 1] = jnp.where(p > pair, second, low)


def direct_kernel(n_col, spots, lists, row_sets, arrived, tiles, parts, mirrored):
    my_row, my_col = lax.axis_index("row"), lax.axis_index("col")
    pair = my_row // 2
    total = jnp.zeros(mirrored.shape, jnp.float32)
    for p in range(arrived.shape[0]):
        both = arrived[spots[p], 0].astype(jnp.float32) + arrived[spots[p], 1].astype(jnp.float32)
        total += jnp.where(p >= pair, both, 0.0)
    mirrored[...] = total
    parts[...] = jnp.zeros_like(parts)
    for k in range(tiles.shape[0]):
        row, col = lists[0, k], lists[1, k]
        here = row_sets[col % 2 * n_col + my_col]
        values = jnp.where(col // 2 == pair, here, arrived[spots[col // 2], col % 2])
        product = lax.dot_general(
            values, tiles[k], (((1,), (1,)), ((), ())), preferred_element_type=jnp.float32
        )
        below = my_row * n_col + row >= col * n_col + my_col
        parts[row] += product * jnp.where(below, 1.0, 0.0)


def body(vectors, tiles, tile_rows, tile_cols, tile_live):
    nvec, seg = vectors.shape
    n_row = lax.axis_size("row")
    n_col = lax.axis_size("col")
    pairs = n_row // 2
    sides = [(i, i ^ 1) for i in range(n_row)]
    order = list(range(pairs))[::-1]
    spots = jnp.array([order.index(p) for p in range(pairs)], jnp.int32)
    params = pltpu.CompilerParams(vmem_limit_bytes=4 << 20)

    near = [[p * 2 * n_col + i for i in range(2 * n_col)] for p in range(pairs)]
    row_sets = exchange(jnp.broadcast_to(vectors[None], (2 * n_col, nvec, seg)), ("row", "col"), near)
    lists = jnp.stack([tile_rows.reshape(-1), tile_cols.reshape(-1), tile_live.reshape(-1)])
    other_lists = lax.ppermute(lists, "row", sides)
    blocks = tiles.reshape(-1, 128, 128)
    other_blocks = lax.ppermute(blocks, "row", sides)
    live = (tile_live.reshape(-1, 1, 1) == 1).astype(tiles.dtype)
    blocks = blocks * live

    outgoing = pl.pallas_call(
        lambda *refs: mirror_kernel(n_col, *refs),
        out_shape=jax.ShapeDtypeStruct((pairs, 2, nvec, seg), jnp.bfloat16),
        in_specs=[SMEM] * 3 + [VMEM] * 3,
        out_specs=VMEM,
        scratch_shapes=[pltpu.VMEM((pairs, nvec, seg), jnp.float32)],
        compiler_params=params,
        name="mirror",
    )(spots, lists, other_lists, row_sets, blocks, other_blocks)
    far = [[2 * p + side for p in order] for side in range(2)]
    arrived = exchange(outgoing, "row", far)
    direct, mirrored = pl.pallas_call(
        lambda *refs: direct_kernel(n_col, *refs),
        out_shape=[
            jax.ShapeDtypeStruct((n_col, nvec, seg), jnp.float32),
            jax.ShapeDtypeStruct((nvec, seg), jnp.float32),
        ],
        in_specs=[SMEM] * 2 + [VMEM] * 3,
        out_specs=[VMEM, VMEM],
        compiler_params=params,
        name="direct",
    )(spots, lists, row_sets, arrived, blocks)
    straight = exchange(direct, "col", None)
    return mirrored + jnp.sum(straight, axis=0)


def solution(mesh):
    return jax.shard_map(
        body,
        mesh=mesh,
        in_specs=(
            P(None, ("row", "col")),
            P("row", "col", None, None, None),
            P("row", "col", None),
            P("row", "col", None),
            P("row", "col", None),
        ),
        out_specs=P(None, ("row", "col")),
        check_vma=False,
    )
```

```python
import jax
import jax.numpy as jnp
from jax import lax
from jax.experimental import pallas as pl
from jax.experimental.pallas import tpu as pltpu
from jax.sharding import PartitionSpec as P

SMEM = pl.BlockSpec(memory_space=pltpu.SMEM)
VMEM = pl.BlockSpec(memory_space=pltpu.VMEM)


def exchange(parts, axes, groups):
    return lax.all_to_all(parts, axes, 0, 0, tiled=True, axis_index_groups=groups)


def stage_kernel(live, tiles, out):
    for k in range(tiles.shape[0]):
        out[k] = jnp.where(live[0, 0, k] == 1, tiles[k], jnp.zeros_like(tiles[k]))


def add_mirror(n_col, who, codes, row_sets, tiles, sums):
    my_row, my_col = lax.axis_index("row"), lax.axis_index("col")
    pair, side = my_row // 2, my_row % 2
    for k in range(tiles.shape[0]):
        row, col = codes[0, k], codes[1, k]
        product = jnp.dot(row_sets[who * n_col + row], tiles[k], preferred_element_type=jnp.float32)
        below = (2 * pair + who) * n_col + row > col * n_col + my_col
        weight = jnp.where(below & (col % 2 == side) & (codes[2, k] == 1), 1.0, 0.0)
        sums[col // 2] += product * weight


def own_kernel(n_col, lists, row_sets, tiles, sums):
    sums[...] = jnp.zeros_like(sums)
    add_mirror(n_col, lax.axis_index("row") % 2, lists, row_sets, tiles, sums)


def pair_kernel(n_col, order, other_lists, row_sets, other_tiles, own_sums, parts, sums):
    my_row, my_col = lax.axis_index("row"), lax.axis_index("col")
    pair = my_row // 2
    sums[...] = own_sums[...]
    add_mirror(n_col, 1 - my_row % 2, other_lists, row_sets, other_tiles, sums)
    first, second = row_sets[my_col], row_sets[n_col + my_col]
    for at, p in enumerate(order):
        high = sums[p].astype(jnp.bfloat16)
        low = (sums[p] - high.astype(jnp.float32)).astype(jnp.bfloat16)
        parts[at, 0] = jnp.where(p > pair, first, high)
        parts[at, 1] = jnp.where(p > pair, second, low)


def direct_kernel(n_col, order, spots, lists, row_sets, arrived, tiles, parts, mirrored):
    my_row, my_col = lax.axis_index("row"), lax.axis_index("col")
    pair = my_row // 2
    total = jnp.zeros(mirrored.shape, jnp.float32)
    for at, p in enumerate(order):
        both = arrived[at, 0].astype(jnp.float32) + arrived[at, 1].astype(jnp.float32)
        total += jnp.where(p >= pair, both, 0.0)
    mirrored[...] = total
    parts[...] = jnp.zeros_like(parts)
    for k in range(tiles.shape[0]):
        row, col = lists[0, k], lists[1, k]
        here = row_sets[col % 2 * n_col + my_col]
        values = jnp.where(col // 2 == pair, here, arrived[spots[col // 2], col % 2])
        product = lax.dot_general(
            values, tiles[k], (((1,), (1,)), ((), ())), preferred_element_type=jnp.float32
        )
        below = my_row * n_col + row >= col * n_col + my_col
        parts[row] += product * jnp.where(below, 1.0, 0.0)


def body(vectors, tiles, tile_rows, tile_cols, tile_live):
    nvec, seg = vectors.shape
    n_row = lax.axis_size("row")
    n_col = lax.axis_size("col")
    pairs = n_row // 2
    sides = [(i, i ^ 1) for i in range(n_row)]
    order = list(range(pairs))[::-1]
    spots = jnp.array([order.index(p) for p in range(pairs)], jnp.int32)
    params = pltpu.CompilerParams(vmem_limit_bytes=4 << 20)

    near = [[p * 2 * n_col + i for i in range(2 * n_col)] for p in range(pairs)]
    row_sets = exchange(jnp.broadcast_to(vectors[None], (2 * n_col, nvec, seg)), ("row", "col"), near)
    lists = jnp.stack([tile_rows.reshape(-1), tile_cols.reshape(-1), tile_live.reshape(-1)])
    other_lists = lax.ppermute(lists, "row", sides)
    blocks = tiles.reshape(-1, 128, 128)
    other_blocks = lax.ppermute(blocks, "row", sides)
    blocks = pl.pallas_call(
        stage_kernel,
        out_shape=jax.ShapeDtypeStruct(blocks.shape, blocks.dtype),
        in_specs=[SMEM, VMEM],
        out_specs=VMEM,
        compiler_params=params,
        cost_estimate=pl.CostEstimate(flops=0, bytes_accessed=4 * blocks.size, transcendentals=0),
        name="stage",
    )(tile_live, blocks)

    own_sums = pl.pallas_call(
        lambda *refs: own_kernel(n_col, *refs),
        out_shape=jax.ShapeDtypeStruct((pairs, nvec, seg), jnp.float32),
        in_specs=[SMEM, VMEM, VMEM],
        out_specs=VMEM,
        compiler_params=params,
        cost_estimate=pl.CostEstimate(flops=10**10, bytes_accessed=2 * blocks.size, transcendentals=0),
        name="own",
    )(lists, row_sets, blocks)
    outgoing = pl.pallas_call(
        lambda *refs: pair_kernel(n_col, order, *refs),
        out_shape=jax.ShapeDtypeStruct((pairs, 2, nvec, seg), jnp.bfloat16),
        in_specs=[SMEM] + [VMEM] * 3,
        out_specs=VMEM,
        scratch_shapes=[pltpu.VMEM((pairs, nvec, seg), jnp.float32)],
        compiler_params=params,
        name="pair",
    )(other_lists, row_sets, other_blocks, own_sums)
    far = [[2 * p + side for p in order] for side in range(2)]
    arrived = exchange(outgoing, "row", far)
    direct, mirrored = pl.pallas_call(
        lambda *refs: direct_kernel(n_col, order, *refs),
        out_shape=[
            jax.ShapeDtypeStruct((n_col, nvec, seg), jnp.float32),
            jax.ShapeDtypeStruct((nvec, seg), jnp.float32),
        ],
        in_specs=[SMEM] * 2 + [VMEM] * 3,
        out_specs=[VMEM, VMEM],
        compiler_params=params,
        name="direct",
    )(spots, lists, row_sets, arrived, blocks)
    straight = exchange(direct, "col", None)
    return mirrored + jnp.sum(straight, axis=0)


def solution(mesh):
    return jax.shard_map(
        body,
        mesh=mesh,
        in_specs=(
            P(None, ("row", "col")),
            P("row", "col", None, None, None),
            P("row", "col", None),
            P("row", "col", None),
            P("row", "col", None),
        ),
        out_specs=P(None, ("row", "col")),
        check_vma=False,
    )
```

```python
import jax
import jax.numpy as jnp
from jax import lax
from jax.experimental import pallas as pl
from jax.experimental.pallas import tpu as pltpu
from jax.sharding import PartitionSpec as P

SMEM = pl.BlockSpec(memory_space=pltpu.SMEM)
VMEM = pl.BlockSpec(memory_space=pltpu.VMEM)


def exchange(parts, axes, groups):
    return lax.all_to_all(parts, axes, 0, 0, tiled=True, axis_index_groups=groups)


def stage_kernel(lists, tiles, out, notes, sem):
    count = tiles.shape[0]
    notes[...] = jnp.zeros_like(notes)
    notes[pl.ds(0, lists.shape[0]), pl.ds(0, count)] = lists[...].astype(jnp.float32)
    out[count] = notes[...].astype(out.dtype)
    copy = pltpu.make_async_copy(tiles, out.at[pl.ds(0, count)], sem)
    copy.start()
    copy.wait()


def add_mirror(n_col, who, slot, count, row_sets, tiles, sums):
    my_row, my_col = lax.axis_index("row"), lax.axis_index("col")
    pair, side = my_row // 2, my_row % 2
    for k in range(count):
        row, col, live = slot(k)
        product = jnp.dot(row_sets[who * n_col + row], tiles[k], preferred_element_type=jnp.float32)
        below = (2 * pair + who) * n_col + row > col * n_col + my_col
        weight = jnp.where(below & (col % 2 == side) & (live == 1), 1.0, 0.0)
        sums[col // 2] += product * weight


def own_kernel(n_col, lists, row_sets, staged, sums):
    sums[...] = jnp.zeros_like(sums)
    slot = lambda k: (lists[0, k], lists[1, k], lists[2, k])
    add_mirror(n_col, lax.axis_index("row") % 2, slot, lists.shape[1], row_sets, staged, sums)


def pair_kernel(n_col, order, row_sets, other, own_sums, parts, sums, page, notes, sem):
    count = other.shape[0] - 1
    page[...] = other[count, pl.ds(0, page.shape[0]), :].astype(jnp.float32).astype(jnp.int32)
    copy = pltpu.make_async_copy(page, notes, sem)
    copy.start()
    my_row, my_col = lax.axis_index("row"), lax.axis_index("col")
    pair = my_row // 2
    sums[...] = own_sums[...]
    copy.wait()
    slot = lambda k: (notes[0, k], notes[1, k], notes[2, k])
    add_mirror(n_col, 1 - my_row % 2, slot, count, row_sets, other, sums)
    first, second = row_sets[my_col], row_sets[n_col + my_col]
    for at, p in enumerate(order):
        high = sums[p].astype(jnp.bfloat16)
        low = (sums[p] - high.astype(jnp.float32)).astype(jnp.bfloat16)
        parts[at, 0] = jnp.where(p > pair, first, high)
        parts[at, 1] = jnp.where(p > pair, second, low)


def direct_kernel(n_col, order, spots, lists, row_sets, arrived, staged, parts, mirrored):
    my_row, my_col = lax.axis_index("row"), lax.axis_index("col")
    pair = my_row // 2
    total = jnp.zeros(mirrored.shape, jnp.float32)
    for at, p in enumerate(order):
        both = arrived[at, 0].astype(jnp.float32) + arrived[at, 1].astype(jnp.float32)
        total += jnp.where(p >= pair, both, 0.0)
    mirrored[...] = total
    parts[...] = jnp.zeros_like(parts)
    for k in range(lists.shape[1]):
        row, col = lists[0, k], lists[1, k]
        here = row_sets[col % 2 * n_col + my_col]
        values = jnp.where(col // 2 == pair, here, arrived[spots[col // 2], col % 2])
        product = lax.dot_general(
            values, staged[k], (((1,), (1,)), ((), ())), preferred_element_type=jnp.float32
        )
        below = my_row * n_col + row >= col * n_col + my_col
        parts[row] += product * jnp.where(below & (lists[2, k] == 1), 1.0, 0.0)


def body(vectors, tiles, tile_rows, tile_cols, tile_live):
    nvec, seg = vectors.shape
    n_row = lax.axis_size("row")
    n_col = lax.axis_size("col")
    pairs = n_row // 2
    sides = [(i, i ^ 1) for i in range(n_row)]
    order = list(range(pairs))[::-1]
    spots = jnp.array([order.index(p) for p in range(pairs)], jnp.int32)
    params = pltpu.CompilerParams(vmem_limit_bytes=4 << 20)

    near = [[p * 2 * n_col + i for i in range(2 * n_col)] for p in range(pairs)]
    row_sets = exchange(jnp.broadcast_to(vectors[None], (2 * n_col, nvec, seg)), ("row", "col"), near)
    blocks = tiles.reshape(-1, 128, 128)
    count = blocks.shape[0]
    lists = jnp.stack([slots.reshape(-1) for slots in (tile_rows, tile_cols, tile_live)])
    staged = pl.pallas_call(
        stage_kernel,
        out_shape=jax.ShapeDtypeStruct((count + 1, 128, 128), blocks.dtype),
        in_specs=[VMEM] * 2,
        out_specs=VMEM,
        scratch_shapes=[pltpu.VMEM((128, 128), jnp.float32), pltpu.SemaphoreType.DMA],
        compiler_params=params,
        cost_estimate=pl.CostEstimate(flops=0, bytes_accessed=4 * blocks.size, transcendentals=0),
        name="stage",
    )(lists, blocks)
    other = lax.ppermute(staged, "row", sides)

    own_sums = pl.pallas_call(
        lambda *refs: own_kernel(n_col, *refs),
        out_shape=jax.ShapeDtypeStruct((pairs, nvec, seg), jnp.float32),
        in_specs=[SMEM] + [VMEM] * 2,
        out_specs=VMEM,
        compiler_params=params,
        cost_estimate=pl.CostEstimate(flops=10**11, bytes_accessed=2 * blocks.size, transcendentals=0),
        name="own",
    )(lists, row_sets, staged)
    outgoing = pl.pallas_call(
        lambda *refs: pair_kernel(n_col, order, *refs),
        out_shape=jax.ShapeDtypeStruct((pairs, 2, nvec, seg), jnp.bfloat16),
        in_specs=[VMEM] * 3,
        out_specs=VMEM,
        scratch_shapes=[
            pltpu.VMEM((pairs, nvec, seg), jnp.float32),
            pltpu.VMEM((16, 128), jnp.int32),
            pltpu.SMEM((16, 128), jnp.int32),
            pltpu.SemaphoreType.DMA,
        ],
        compiler_params=params,
        name="pair",
    )(row_sets, other, own_sums)
    far = [[2 * p + side for p in order] for side in range(2)]
    arrived = exchange(outgoing, "row", far)
    direct, mirrored = pl.pallas_call(
        lambda *refs: direct_kernel(n_col, order, *refs),
        out_shape=[
            jax.ShapeDtypeStruct((n_col, nvec, seg), jnp.float32),
            jax.ShapeDtypeStruct((nvec, seg), jnp.float32),
        ],
        in_specs=[SMEM] * 2 + [VMEM] * 3,
        out_specs=[VMEM, VMEM],
        compiler_params=params,
        name="direct",
    )(spots, lists, row_sets, arrived, staged)
    straight = exchange(direct, "col", None)
    return mirrored + jnp.sum(straight, axis=0)


def solution(mesh):
    return jax.shard_map(
        body,
        mesh=mesh,
        in_specs=(
            P(None, ("row", "col")),
            P("row", "col", None, None, None),
            P("row", "col", None),
            P("row", "col", None),
            P("row", "col", None),
        ),
        out_specs=P(None, ("row", "col")),
        check_vma=False,
    )
```

```python
import jax
import jax.numpy as jnp
from jax import lax
from jax.experimental import pallas as pl
from jax.experimental.pallas import tpu as pltpu
from jax.sharding import PartitionSpec as P

SMEM = pl.BlockSpec(memory_space=pltpu.SMEM)
VMEM = pl.BlockSpec(memory_space=pltpu.VMEM)


def exchange(parts, axes, groups):
    return lax.all_to_all(parts, axes, 0, 0, tiled=True, axis_index_groups=groups)


def seat(col, n_col):
    y, half = col // 2, n_col // 4
    return y % half * 4 + y // half * 2 + col % 2


def plane_order(planes):
    anchor = planes * 3 // 4
    apart = lambda z: min((z - anchor) % planes, (anchor - z) % planes)
    return [1, 0] + sorted(range(2, planes), key=apart)


def stage_kernel(lists, tiles, out, notes, sem):
    count = tiles.shape[0]
    notes[...] = jnp.zeros_like(notes)
    notes[pl.ds(0, lists.shape[0]), pl.ds(0, count)] = lists[...].astype(jnp.float32)
    out[count] = notes[...].astype(out.dtype)
    copy = pltpu.make_async_copy(tiles, out.at[pl.ds(0, count)], sem)
    copy.start()
    copy.wait()


def add_mirror(n_col, who, slot, count, row_sets, tiles, sums):
    my_row, my_col = lax.axis_index("row"), lax.axis_index("col")
    pair, side = my_row // 2, my_row % 2
    for k in range(count):
        row, col, live = slot(k)
        product = jnp.dot(row_sets[seat(row, n_col) * 2 + who], tiles[k], preferred_element_type=jnp.float32)
        below = (2 * pair + who) * n_col + row > col * n_col + my_col
        weight = jnp.where(below & (col % 2 == side) & (live == 1), 1.0, 0.0)
        sums[col // 2] += product * weight


def own_kernel(n_col, lists, row_sets, staged, sums):
    sums[...] = jnp.zeros_like(sums)
    slot = lambda k: (lists[0, k], lists[1, k], lists[2, k])
    add_mirror(n_col, lax.axis_index("row") % 2, slot, lists.shape[1], row_sets, staged, sums)


def pair_kernel(n_col, order, row_sets, other, own_sums, parts, sums, page, notes, sem):
    count = other.shape[0] - 1
    page[...] = other[count, pl.ds(0, page.shape[0]), :].astype(jnp.float32).astype(jnp.int32)
    copy = pltpu.make_async_copy(page, notes, sem)
    copy.start()
    my_row, my_col = lax.axis_index("row"), lax.axis_index("col")
    pair = my_row // 2
    sums[...] = own_sums[...]
    copy.wait()
    slot = lambda k: (notes[0, k], notes[1, k], notes[2, k])
    add_mirror(n_col, 1 - my_row % 2, slot, count, row_sets, other, sums)
    first, second = row_sets[seat(my_col, n_col) * 2], row_sets[seat(my_col, n_col) * 2 + 1]
    for at, p in enumerate(order):
        high = sums[p].astype(jnp.bfloat16)
        low = (sums[p] - high.astype(jnp.float32)).astype(jnp.bfloat16)
        parts[at, 0] = jnp.where(p > pair, first, high)
        parts[at, 1] = jnp.where(p > pair, second, low)


def direct_kernel(n_col, order, spots, lists, row_sets, arrived, staged, parts, mirrored):
    my_row, my_col = lax.axis_index("row"), lax.axis_index("col")
    pair = my_row // 2
    total = jnp.zeros(mirrored.shape, jnp.float32)
    for at, p in enumerate(order):
        both = arrived[at, 0].astype(jnp.float32) + arrived[at, 1].astype(jnp.float32)
        total += jnp.where(p >= pair, both, 0.0)
    mirrored[...] = total
    parts[...] = jnp.zeros_like(parts)
    for k in range(lists.shape[1]):
        row, col = lists[0, k], lists[1, k]
        here = row_sets[seat(my_col, n_col) * 2 + col % 2]
        values = jnp.where(col // 2 == pair, here, arrived[spots[col // 2], col % 2])
        product = lax.dot_general(
            values, staged[k], (((1,), (1,)), ((), ())), preferred_element_type=jnp.float32
        )
        below = my_row * n_col + row >= col * n_col + my_col
        parts[seat(row, n_col)] += product * jnp.where(below & (lists[2, k] == 1), 1.0, 0.0)


def body(vectors, tiles, tile_rows, tile_cols, tile_live):
    nvec, seg = vectors.shape
    n_row = lax.axis_size("row")
    n_col = lax.axis_size("col")
    pairs = n_row // 2
    sides = [(i, i ^ 1) for i in range(n_row)]
    order = [2 * z + half for z in plane_order(pairs // 2) for half in (1, 0)]
    spots = jnp.array([order.index(p) for p in range(pairs)], jnp.int32)
    params = pltpu.CompilerParams(vmem_limit_bytes=4 << 20)

    columns = sorted(range(n_col), key=lambda c: seat(c, n_col))
    near = [[(2 * p + side) * n_col + c for c in columns for side in range(2)] for p in range(pairs)]
    row_sets = exchange(jnp.broadcast_to(vectors[None], (2 * n_col, nvec, seg)), ("row", "col"), near)
    blocks = tiles.reshape(-1, 128, 128)
    count = blocks.shape[0]
    lists = jnp.stack([slots.reshape(-1) for slots in (tile_rows, tile_cols, tile_live)])
    staged = pl.pallas_call(
        stage_kernel,
        out_shape=jax.ShapeDtypeStruct((count + 1, 128, 128), blocks.dtype),
        in_specs=[VMEM] * 2,
        out_specs=VMEM,
        scratch_shapes=[pltpu.VMEM((128, 128), jnp.float32), pltpu.SemaphoreType.DMA],
        compiler_params=params,
        cost_estimate=pl.CostEstimate(flops=0, bytes_accessed=4 * blocks.size, transcendentals=0),
        name="stage",
    )(lists, blocks)
    other = lax.ppermute(staged, "row", sides)

    own_sums = pl.pallas_call(
        lambda *refs: own_kernel(n_col, *refs),
        out_shape=jax.ShapeDtypeStruct((pairs, nvec, seg), jnp.float32),
        in_specs=[SMEM] + [VMEM] * 2,
        out_specs=VMEM,
        compiler_params=params,
        cost_estimate=pl.CostEstimate(flops=10**11, bytes_accessed=2 * blocks.size, transcendentals=0),
        name="own",
    )(lists, row_sets, staged)
    outgoing = pl.pallas_call(
        lambda *refs: pair_kernel(n_col, order, *refs),
        out_shape=jax.ShapeDtypeStruct((pairs, 2, nvec, seg), jnp.bfloat16),
        in_specs=[VMEM] * 3,
        out_specs=VMEM,
        scratch_shapes=[
            pltpu.VMEM((pairs, nvec, seg), jnp.float32),
            pltpu.VMEM((16, 128), jnp.int32),
            pltpu.SMEM((16, 128), jnp.int32),
            pltpu.SemaphoreType.DMA,
        ],
        compiler_params=params,
        name="pair",
    )(row_sets, other, own_sums)
    far = [[2 * p + side for p in order] for side in range(2)]
    arrived = exchange(outgoing, "row", far)
    direct, mirrored = pl.pallas_call(
        lambda *refs: direct_kernel(n_col, order, *refs),
        out_shape=[
            jax.ShapeDtypeStruct((n_col, nvec, seg), jnp.float32),
            jax.ShapeDtypeStruct((nvec, seg), jnp.float32),
        ],
        in_specs=[SMEM] * 2 + [VMEM] * 3,
        out_specs=[VMEM, VMEM],
        compiler_params=params,
        name="direct",
    )(spots, lists, row_sets, arrived, staged)
    straight = exchange(direct, "col", [columns])
    return mirrored + jnp.sum(straight, axis=0)


def solution(mesh):
    return jax.shard_map(
        body,
        mesh=mesh,
        in_specs=(
            P(None, ("row", "col")),
            P("row", "col", None, None, None),
            P("row", "col", None),
            P("row", "col", None),
            P("row", "col", None),
        ),
        out_specs=P(None, ("row", "col")),
        check_vma=False,
    )
```

```python
import jax
import jax.numpy as jnp
from jax import lax
from jax.experimental import pallas as pl
from jax.experimental.pallas import tpu as pltpu
from jax.sharding import PartitionSpec as P

SMEM = pl.BlockSpec(memory_space=pltpu.SMEM)
VMEM = pl.BlockSpec(memory_space=pltpu.VMEM)


def exchange(parts, axes, groups):
    return lax.all_to_all(parts, axes, 0, 0, tiled=True, axis_index_groups=groups)


def stage_kernel(lists, tiles, out, notes, sem):
    count = tiles.shape[0]
    notes[...] = jnp.zeros_like(notes)
    notes[pl.ds(0, lists.shape[0]), pl.ds(0, count)] = lists[...].astype(jnp.float32)
    out[count] = notes[...].astype(out.dtype)
    copy = pltpu.make_async_copy(tiles, out.at[pl.ds(0, count)], sem)
    copy.start()
    copy.wait()


def add_mirror(n_col, who, slot, count, row_sets, tiles, sums):
    my_row, my_col = lax.axis_index("row"), lax.axis_index("col")
    pair, side = my_row // 2, my_row % 2
    for k in range(count):
        row, col, live = slot(k)
        product = jnp.dot(row_sets[who * n_col + row], tiles[k], preferred_element_type=jnp.float32)
        below = (2 * pair + who) * n_col + row > col * n_col + my_col
        weight = jnp.where(below & (col % 2 == side) & (live == 1), 1.0, 0.0)
        sums[col // 2] += product * weight


def own_kernel(n_col, lists, row_sets, staged, sums):
    sums[...] = jnp.zeros_like(sums)
    slot = lambda k: (lists[0, k], lists[1, k], lists[2, k])
    add_mirror(n_col, lax.axis_index("row") % 2, slot, lists.shape[1], row_sets, staged, sums)


def pair_kernel(n_col, order, row_sets, other, own_sums, parts, sums, page, notes, sem):
    count = other.shape[0] - 1
    page[...] = other[count, pl.ds(0, page.shape[0]), :].astype(jnp.float32).astype(jnp.int32)
    copy = pltpu.make_async_copy(page, notes, sem)
    copy.start()
    my_row, my_col = lax.axis_index("row"), lax.axis_index("col")
    pair = my_row // 2
    sums[...] = own_sums[...]
    copy.wait()
    slot = lambda k: (notes[0, k], notes[1, k], notes[2, k])
    add_mirror(n_col, 1 - my_row % 2, slot, count, row_sets, other, sums)
    first, second = row_sets[my_col], row_sets[n_col + my_col]
    for at, p in enumerate(order):
        high = sums[p].astype(jnp.bfloat16)
        low = (sums[p] - high.astype(jnp.float32)).astype(jnp.bfloat16)
        parts[at, 0] = jnp.where(p > pair, first, high)
        parts[at, 1] = jnp.where(p > pair, second, low)


def direct_kernel(n_col, order, spots, lists, row_sets, arrived, staged, parts, mirrored):
    my_row, my_col = lax.axis_index("row"), lax.axis_index("col")
    pair = my_row // 2
    total = jnp.zeros(mirrored.shape, jnp.float32)
    for at, p in enumerate(order):
        both = arrived[at, 0].astype(jnp.float32) + arrived[at, 1].astype(jnp.float32)
        total += jnp.where(p >= pair, both, 0.0)
    mirrored[...] = total
    parts[...] = jnp.zeros_like(parts)
    for k in range(lists.shape[1]):
        row, col = lists[0, k], lists[1, k]
        here = row_sets[col % 2 * n_col + my_col]
        values = jnp.where(col // 2 == pair, here, arrived[spots[col // 2], col % 2])
        product = lax.dot_general(
            values, staged[k], (((1,), (1,)), ((), ())), preferred_element_type=jnp.float32
        )
        below = my_row * n_col + row >= col * n_col + my_col
        parts[row] += product * jnp.where(below & (lists[2, k] == 1), 1.0, 0.0)


def body(vectors, tiles, tile_rows, tile_cols, tile_live):
    nvec, seg = vectors.shape
    n_row = lax.axis_size("row")
    n_col = lax.axis_size("col")
    pairs = n_row // 2
    sides = [(i, i ^ 1) for i in range(n_row)]
    planes = pairs // 2
    order = [2 * (i * (planes // 2 + 1) % planes) + half for i in range(planes) for half in range(2)]
    spots = jnp.array([order.index(p) for p in range(pairs)], jnp.int32)
    params = pltpu.CompilerParams(vmem_limit_bytes=4 << 20)

    near = [[p * 2 * n_col + i for i in range(2 * n_col)] for p in range(pairs)]
    row_sets = exchange(jnp.broadcast_to(vectors[None], (2 * n_col, nvec, seg)), ("row", "col"), near)
    blocks = tiles.reshape(-1, 128, 128)
    count = blocks.shape[0]
    lists = jnp.stack([slots.reshape(-1) for slots in (tile_rows, tile_cols, tile_live)])
    staged = pl.pallas_call(
        stage_kernel,
        out_shape=jax.ShapeDtypeStruct((count + 1, 128, 128), blocks.dtype),
        in_specs=[VMEM] * 2,
        out_specs=VMEM,
        scratch_shapes=[pltpu.VMEM((128, 128), jnp.float32), pltpu.SemaphoreType.DMA],
        compiler_params=params,
        cost_estimate=pl.CostEstimate(flops=0, bytes_accessed=4 * blocks.size, transcendentals=0),
        name="stage",
    )(lists, blocks)
    other = lax.ppermute(staged, "row", sides)

    own_sums = pl.pallas_call(
        lambda *refs: own_kernel(n_col, *refs),
        out_shape=jax.ShapeDtypeStruct((pairs, nvec, seg), jnp.float32),
        in_specs=[SMEM] + [VMEM] * 2,
        out_specs=VMEM,
        compiler_params=params,
        cost_estimate=pl.CostEstimate(flops=10**11, bytes_accessed=2 * blocks.size, transcendentals=0),
        name="own",
    )(lists, row_sets, staged)
    outgoing = pl.pallas_call(
        lambda *refs: pair_kernel(n_col, order, *refs),
        out_shape=jax.ShapeDtypeStruct((pairs, 2, nvec, seg), jnp.bfloat16),
        in_specs=[VMEM] * 3,
        out_specs=VMEM,
        scratch_shapes=[
            pltpu.VMEM((pairs, nvec, seg), jnp.float32),
            pltpu.VMEM((16, 128), jnp.int32),
            pltpu.SMEM((16, 128), jnp.int32),
            pltpu.SemaphoreType.DMA,
        ],
        compiler_params=params,
        name="pair",
    )(row_sets, other, own_sums)
    far = [[2 * p + side for p in order] for side in range(2)]
    arrived = exchange(outgoing, "row", far)
    direct, mirrored = pl.pallas_call(
        lambda *refs: direct_kernel(n_col, order, *refs),
        out_shape=[
            jax.ShapeDtypeStruct((n_col, nvec, seg), jnp.float32),
            jax.ShapeDtypeStruct((nvec, seg), jnp.float32),
        ],
        in_specs=[SMEM] * 2 + [VMEM] * 3,
        out_specs=[VMEM, VMEM],
        compiler_params=params,
        name="direct",
    )(spots, lists, row_sets, arrived, staged)
    straight = exchange(direct, "col", None)
    return mirrored + jnp.sum(straight, axis=0)


def solution(mesh):
    return jax.shard_map(
        body,
        mesh=mesh,
        in_specs=(
            P(None, ("row", "col")),
            P("row", "col", None, None, None),
            P("row", "col", None),
            P("row", "col", None),
            P("row", "col", None),
        ),
        out_specs=P(None, ("row", "col")),
        check_vma=False,
    )
```

```python
import jax
import jax.numpy as jnp
from jax import lax
from jax.experimental import pallas as pl
from jax.experimental.pallas import tpu as pltpu
from jax.sharding import PartitionSpec as P

SMEM = pl.BlockSpec(memory_space=pltpu.SMEM)
VMEM = pl.BlockSpec(memory_space=pltpu.VMEM)


def exchange(parts, axes, groups):
    return lax.all_to_all(parts, axes, 0, 0, tiled=True, axis_index_groups=groups)


def stage_kernel(lists, tiles, out, notes, sem):
    count = tiles.shape[0]
    notes[...] = jnp.zeros_like(notes)
    notes[pl.ds(0, lists.shape[0]), pl.ds(0, count)] = lists[...].astype(jnp.float32)
    out[count] = notes[...].astype(out.dtype)
    copy = pltpu.make_async_copy(tiles, out.at[pl.ds(0, count)], sem)
    copy.start()
    copy.wait()


def add_mirror(n_col, who, slot, count, row_sets, tiles, sums):
    my_row, my_col = lax.axis_index("row"), lax.axis_index("col")
    pair, side = my_row // 2, my_row % 2
    for k in range(count):
        row, col, live = slot(k)
        product = jnp.dot(row_sets[who * n_col + row], tiles[k], preferred_element_type=jnp.float32)
        below = (2 * pair + who) * n_col + row > col * n_col + my_col
        weight = jnp.where(below & (col % 2 == side) & (live == 1), 1.0, 0.0)
        sums[col // 2] += product * weight


def own_kernel(n_col, lists, row_sets, staged, sums):
    sums[...] = jnp.zeros_like(sums)
    slot = lambda k: (lists[0, k], lists[1, k], lists[2, k])
    add_mirror(n_col, lax.axis_index("row") % 2, slot, lists.shape[1], row_sets, staged, sums)


def pair_kernel(n_col, order, row_sets, other, own_sums, parts, sums, page, notes, sem):
    count = other.shape[0] - 1
    page[...] = other[count, pl.ds(0, page.shape[0]), :].astype(jnp.float32).astype(jnp.int32)
    copy = pltpu.make_async_copy(page, notes, sem)
    copy.start()
    my_row, my_col = lax.axis_index("row"), lax.axis_index("col")
    pair = my_row // 2
    sums[...] = own_sums[...]
    copy.wait()
    slot = lambda k: (notes[0, k], notes[1, k], notes[2, k])
    add_mirror(n_col, 1 - my_row % 2, slot, count, row_sets, other, sums)
    first, second = row_sets[my_col], row_sets[n_col + my_col]
    for at, p in enumerate(order):
        high = sums[p].astype(jnp.bfloat16)
        low = (sums[p] - high.astype(jnp.float32)).astype(jnp.bfloat16)
        parts[at, 0] = jnp.where(p > pair, first, high)
        parts[at, 1] = jnp.where(p > pair, second, low)


def direct_kernel(n_col, order, spots, lists, row_sets, arrived, staged, parts, mirrored):
    my_row, my_col = lax.axis_index("row"), lax.axis_index("col")
    pair = my_row // 2
    total = jnp.zeros(mirrored.shape, jnp.float32)
    for at, p in enumerate(order):
        both = arrived[at, 0].astype(jnp.float32) + arrived[at, 1].astype(jnp.float32)
        total += jnp.where(p >= pair, both, 0.0)
    mirrored[...] = total
    parts[...] = jnp.zeros_like(parts)
    for k in range(lists.shape[1]):
        row, col = lists[0, k], lists[1, k]
        here = row_sets[col % 2 * n_col + my_col]
        values = jnp.where(col // 2 == pair, here, arrived[spots[col // 2], col % 2])
        product = lax.dot_general(
            values, staged[k], (((1,), (1,)), ((), ())), preferred_element_type=jnp.float32
        )
        below = my_row * n_col + row >= col * n_col + my_col
        parts[row] += product * jnp.where(below & (lists[2, k] == 1), 1.0, 0.0)


def body(vectors, tiles, tile_rows, tile_cols, tile_live):
    nvec, seg = vectors.shape
    n_row = lax.axis_size("row")
    n_col = lax.axis_size("col")
    pairs = n_row // 2
    sides = [(i, i ^ 1) for i in range(n_row)]
    planes = pairs // 2
    order = [2 * (i * (planes // 2 - 1) % planes) + half for i in range(planes) for half in (1, 0)]
    spots = jnp.array([order.index(p) for p in range(pairs)], jnp.int32)
    params = pltpu.CompilerParams(vmem_limit_bytes=4 << 20)

    near = [[p * 2 * n_col + i for i in range(2 * n_col)] for p in range(pairs)]
    row_sets = exchange(jnp.broadcast_to(vectors[None], (2 * n_col, nvec, seg)), ("row", "col"), near)
    blocks = tiles.reshape(-1, 128, 128)
    count = blocks.shape[0]
    lists = jnp.stack([slots.reshape(-1) for slots in (tile_rows, tile_cols, tile_live)])
    staged = pl.pallas_call(
        stage_kernel,
        out_shape=jax.ShapeDtypeStruct((count + 1, 128, 128), blocks.dtype),
        in_specs=[VMEM] * 2,
        out_specs=VMEM,
        scratch_shapes=[pltpu.VMEM((128, 128), jnp.float32), pltpu.SemaphoreType.DMA],
        compiler_params=params,
        cost_estimate=pl.CostEstimate(flops=0, bytes_accessed=4 * blocks.size, transcendentals=0),
        name="stage",
    )(lists, blocks)
    other = lax.ppermute(staged, "row", sides)

    own_sums = pl.pallas_call(
        lambda *refs: own_kernel(n_col, *refs),
        out_shape=jax.ShapeDtypeStruct((pairs, nvec, seg), jnp.float32),
        in_specs=[SMEM] + [VMEM] * 2,
        out_specs=VMEM,
        compiler_params=params,
        cost_estimate=pl.CostEstimate(flops=10**11, bytes_accessed=2 * blocks.size, transcendentals=0),
        name="own",
    )(lists, row_sets, staged)
    outgoing = pl.pallas_call(
        lambda *refs: pair_kernel(n_col, order, *refs),
        out_shape=jax.ShapeDtypeStruct((pairs, 2, nvec, seg), jnp.bfloat16),
        in_specs=[VMEM] * 3,
        out_specs=VMEM,
        scratch_shapes=[
            pltpu.VMEM((pairs, nvec, seg), jnp.float32),
            pltpu.VMEM((16, 128), jnp.int32),
            pltpu.SMEM((16, 128), jnp.int32),
            pltpu.SemaphoreType.DMA,
        ],
        compiler_params=params,
        name="pair",
    )(row_sets, other, own_sums)
    far = [[2 * p + side for p in order] for side in range(2)]
    arrived = exchange(outgoing, "row", far)
    direct, mirrored = pl.pallas_call(
        lambda *refs: direct_kernel(n_col, order, *refs),
        out_shape=[
            jax.ShapeDtypeStruct((n_col, nvec, seg), jnp.float32),
            jax.ShapeDtypeStruct((nvec, seg), jnp.float32),
        ],
        in_specs=[SMEM] * 2 + [VMEM] * 3,
        out_specs=[VMEM, VMEM],
        compiler_params=params,
        name="direct",
    )(spots, lists, row_sets, arrived, staged)
    straight = exchange(direct, "col", None)
    return mirrored + jnp.sum(straight, axis=0)


def solution(mesh):
    return jax.shard_map(
        body,
        mesh=mesh,
        in_specs=(
            P(None, ("row", "col")),
            P("row", "col", None, None, None),
            P("row", "col", None),
            P("row", "col", None),
            P("row", "col", None),
        ),
        out_specs=P(None, ("row", "col")),
        check_vma=False,
    )
```

```python
import jax
import jax.numpy as jnp
from jax import lax
from jax.experimental import pallas as pl
from jax.experimental.pallas import tpu as pltpu
from jax.sharding import PartitionSpec as P

SMEM = pl.BlockSpec(memory_space=pltpu.SMEM)
VMEM = pl.BlockSpec(memory_space=pltpu.VMEM)


def exchange(parts, axes, groups):
    return lax.all_to_all(parts, axes, 0, 0, tiled=True, axis_index_groups=groups)


def seat(col, n_col):
    half = n_col // 4
    y = col >> 1
    return ((y & (half - 1)) << 2) | ((y >> (half.bit_length() - 1)) << 1) | (col & 1)


def stage_kernel(lists, tiles, out, notes, sem):
    count = tiles.shape[0]
    notes[...] = jnp.zeros_like(notes)
    notes[pl.ds(0, lists.shape[0]), pl.ds(0, count)] = lists[...].astype(jnp.float32)
    out[count] = notes[...].astype(out.dtype)
    copy = pltpu.make_async_copy(tiles, out.at[pl.ds(0, count)], sem)
    copy.start()
    copy.wait()


def add_mirror(n_col, who, slot, count, row_sets, tiles, sums):
    my_row, my_col = lax.axis_index("row"), lax.axis_index("col")
    pair, side = my_row >> 1, my_row & 1
    for k in range(count):
        row, col, live = slot(k)
        product = jnp.dot(row_sets[(seat(row, n_col) << 1) | who], tiles[k], preferred_element_type=jnp.float32)
        below = (2 * pair + who) * n_col + row > col * n_col + my_col
        weight = jnp.where(below & ((col & 1) == side) & (live == 1), 1.0, 0.0)
        sums[col >> 1] += product * weight


def own_kernel(n_col, lists, row_sets, staged, sums):
    sums[...] = jnp.zeros_like(sums)
    slot = lambda k: (lists[0, k], lists[1, k], lists[2, k])
    add_mirror(n_col, lax.axis_index("row") & 1, slot, lists.shape[1], row_sets, staged, sums)


def pair_kernel(n_col, order, row_sets, other, own_sums, parts, sums, page, notes, sem):
    count = other.shape[0] - 1
    page[...] = other[count, pl.ds(0, page.shape[0]), :].astype(jnp.float32).astype(jnp.int32)
    copy = pltpu.make_async_copy(page, notes, sem)
    copy.start()
    my_row, my_col = lax.axis_index("row"), lax.axis_index("col")
    pair = my_row >> 1
    sums[...] = own_sums[...]
    copy.wait()
    slot = lambda k: (notes[0, k], notes[1, k], notes[2, k])
    add_mirror(n_col, 1 - (my_row & 1), slot, count, row_sets, other, sums)
    first, second = row_sets[seat(my_col, n_col) << 1], row_sets[(seat(my_col, n_col) << 1) | 1]
    for at, p in enumerate(order):
        high = sums[p].astype(jnp.bfloat16)
        low = (sums[p] - high.astype(jnp.float32)).astype(jnp.bfloat16)
        parts[at, 0] = jnp.where(p > pair, first, high)
        parts[at, 1] = jnp.where(p > pair, second, low)


def direct_kernel(n_col, order, spots, lists, row_sets, arrived, staged, parts, mirrored):
    my_row, my_col = lax.axis_index("row"), lax.axis_index("col")
    pair = my_row >> 1
    total = jnp.zeros(mirrored.shape, jnp.float32)
    for at, p in enumerate(order):
        both = arrived[at, 0].astype(jnp.float32) + arrived[at, 1].astype(jnp.float32)
        total += jnp.where(p >= pair, both, 0.0)
    mirrored[...] = total
    parts[...] = jnp.zeros_like(parts)
    base = seat(my_col, n_col) << 1
    for k in range(lists.shape[1]):
        row, col = lists[0, k], lists[1, k]
        here = row_sets[base + (col & 1)]
        values = jnp.where((col >> 1) == pair, here, arrived[spots[col >> 1], col & 1])
        product = lax.dot_general(
            values, staged[k], (((1,), (1,)), ((), ())), preferred_element_type=jnp.float32
        )
        below = my_row * n_col + row >= col * n_col + my_col
        parts[row] += product * jnp.where(below & (lists[2, k] == 1), 1.0, 0.0)


def body(vectors, tiles, tile_rows, tile_cols, tile_live):
    nvec, seg = vectors.shape
    n_row = lax.axis_size("row")
    n_col = lax.axis_size("col")
    pairs = n_row // 2
    sides = [(i, i ^ 1) for i in range(n_row)]
    order = list(range(pairs))[::-1]
    spots = jnp.array([order.index(p) for p in range(pairs)], jnp.int32)
    params = pltpu.CompilerParams(vmem_limit_bytes=4 << 20)

    columns = sorted(range(n_col), key=lambda c: seat(c, n_col))
    near = [[(2 * p + side) * n_col + c for c in columns for side in range(2)] for p in range(pairs)]
    row_sets = exchange(jnp.broadcast_to(vectors[None], (2 * n_col, nvec, seg)), ("row", "col"), near)
    blocks = tiles.reshape(-1, 128, 128)
    count = blocks.shape[0]
    lists = jnp.stack([slots.reshape(-1) for slots in (tile_rows, tile_cols, tile_live)])
    staged = pl.pallas_call(
        stage_kernel,
        out_shape=jax.ShapeDtypeStruct((count + 1, 128, 128), blocks.dtype),
        in_specs=[VMEM] * 2,
        out_specs=VMEM,
        scratch_shapes=[pltpu.VMEM((128, 128), jnp.float32), pltpu.SemaphoreType.DMA],
        compiler_params=params,
        cost_estimate=pl.CostEstimate(flops=0, bytes_accessed=4 * blocks.size, transcendentals=0),
        name="stage",
    )(lists, blocks)
    other = lax.ppermute(staged, "row", sides)

    own_sums = pl.pallas_call(
        lambda *refs: own_kernel(n_col, *refs),
        out_shape=jax.ShapeDtypeStruct((pairs, nvec, seg), jnp.float32),
        in_specs=[SMEM] + [VMEM] * 2,
        out_specs=VMEM,
        compiler_params=params,
        cost_estimate=pl.CostEstimate(flops=10**11, bytes_accessed=2 * blocks.size, transcendentals=0),
        name="own",
    )(lists, row_sets, staged)
    outgoing = pl.pallas_call(
        lambda *refs: pair_kernel(n_col, order, *refs),
        out_shape=jax.ShapeDtypeStruct((pairs, 2, nvec, seg), jnp.bfloat16),
        in_specs=[VMEM] * 3,
        out_specs=VMEM,
        scratch_shapes=[
            pltpu.VMEM((pairs, nvec, seg), jnp.float32),
            pltpu.VMEM((16, 128), jnp.int32),
            pltpu.SMEM((16, 128), jnp.int32),
            pltpu.SemaphoreType.DMA,
        ],
        compiler_params=params,
        name="pair",
    )(row_sets, other, own_sums)
    far = [[2 * p + side for p in order] for side in range(2)]
    arrived = exchange(outgoing, "row", far)
    direct, mirrored = pl.pallas_call(
        lambda *refs: direct_kernel(n_col, order, *refs),
        out_shape=[
            jax.ShapeDtypeStruct((n_col, nvec, seg), jnp.float32),
            jax.ShapeDtypeStruct((nvec, seg), jnp.float32),
        ],
        in_specs=[SMEM] * 2 + [VMEM] * 3,
        out_specs=[VMEM, VMEM],
        compiler_params=params,
        name="direct",
    )(spots, lists, row_sets, arrived, staged)
    straight = exchange(direct, "col", None)
    return mirrored + jnp.sum(straight, axis=0)


def solution(mesh):
    return jax.shard_map(
        body,
        mesh=mesh,
        in_specs=(
            P(None, ("row", "col")),
            P("row", "col", None, None, None),
            P("row", "col", None),
            P("row", "col", None),
            P("row", "col", None),
        ),
        out_specs=P(None, ("row", "col")),
        check_vma=False,
    )
```

```python
import jax
import jax.numpy as jnp
from jax import lax
from jax.experimental import pallas as pl
from jax.experimental.pallas import tpu as pltpu
from jax.sharding import PartitionSpec as P

SMEM = pl.BlockSpec(memory_space=pltpu.SMEM)
VMEM = pl.BlockSpec(memory_space=pltpu.VMEM)


def exchange(parts, axes, groups):
    return lax.all_to_all(parts, axes, 0, 0, tiled=True, axis_index_groups=groups)


def seat(col, n_col):
    half = n_col // 4
    y = col >> 1
    return ((y & (half - 1)) << 2) | ((y >> (half.bit_length() - 1)) << 1) | (col & 1)


def stage_kernel(rows, cols, live, tiles, out, page, notes, sems):
    count, pieces = tiles.shape[0], sems.shape[0] - 1
    step = count // pieces
    copies = [
        pltpu.make_async_copy(tiles.at[pl.ds(i * step, step)], out.at[pl.ds(i * step, step)], sems.at[i])
        for i in range(pieces)
    ]
    for copy in copies:
        copy.start()
    notes[...] = jnp.zeros_like(notes)
    for at, slots in enumerate((rows, cols, live)):
        notes[pl.ds(at, 1), pl.ds(0, count)] = slots[0].astype(jnp.float32)
    page[0] = notes[...].astype(page.dtype)
    copies.append(pltpu.make_async_copy(page, out.at[pl.ds(count, 1)], sems.at[pieces]))
    copies[-1].start()
    for copy in copies:
        copy.wait()


def add_mirror(n_col, who, slot, count, row_sets, tiles, sums):
    my_row, my_col = lax.axis_index("row"), lax.axis_index("col")
    pair, side = my_row >> 1, my_row & 1
    for k in range(count):
        row, col, live = slot(k)
        product = jnp.dot(row_sets[(seat(row, n_col) << 1) | who], tiles[k], preferred_element_type=jnp.float32)
        below = (2 * pair + who) * n_col + row > col * n_col + my_col
        weight = jnp.where(below & ((col & 1) == side) & (live == 1), 1.0, 0.0)
        sums[col >> 1] += product * weight


def own_kernel(n_col, rows, cols, live, row_sets, staged, sums):
    sums[...] = jnp.zeros_like(sums)
    slot = lambda k: (rows[0, 0, k], cols[0, 0, k], live[0, 0, k])
    add_mirror(n_col, lax.axis_index("row") & 1, slot, rows.shape[2], row_sets, staged, sums)


def pair_kernel(n_col, order, row_sets, other, own_sums, parts, sums, page, notes, sem):
    count = other.shape[0] - 1
    page[...] = other[count, pl.ds(0, page.shape[0]), :].astype(jnp.float32).astype(jnp.int32)
    copy = pltpu.make_async_copy(page, notes, sem)
    copy.start()
    my_row, my_col = lax.axis_index("row"), lax.axis_index("col")
    pair = my_row >> 1
    sums[...] = own_sums[...]
    copy.wait()
    slot = lambda k: (notes[0, k], notes[1, k], notes[2, k])
    add_mirror(n_col, 1 - (my_row & 1), slot, count, row_sets, other, sums)
    first, second = row_sets[seat(my_col, n_col) << 1], row_sets[(seat(my_col, n_col) << 1) | 1]
    for at, p in enumerate(order):
        high = sums[p].astype(jnp.bfloat16)
        low = (sums[p] - high.astype(jnp.float32)).astype(jnp.bfloat16)
        parts[at, 0] = jnp.where(p > pair, first, high)
        parts[at, 1] = jnp.where(p > pair, second, low)


def direct_kernel(n_col, order, spots, rows, cols, live, row_sets, arrived, staged, parts, mirrored):
    my_row, my_col = lax.axis_index("row"), lax.axis_index("col")
    pair = my_row >> 1
    total = jnp.zeros(mirrored.shape, jnp.float32)
    for at, p in enumerate(order):
        both = arrived[at, 0].astype(jnp.float32) + arrived[at, 1].astype(jnp.float32)
        total += jnp.where(p >= pair, both, 0.0)
    mirrored[...] = total
    parts[...] = jnp.zeros_like(parts)
    base = seat(my_col, n_col) << 1
    for k in range(rows.shape[2]):
        row, col = rows[0, 0, k], cols[0, 0, k]
        here = row_sets[base + (col & 1)]
        values = jnp.where((col >> 1) == pair, here, arrived[spots[col >> 1], col & 1])
        product = lax.dot_general(
            values, staged[k], (((1,), (1,)), ((), ())), preferred_element_type=jnp.float32
        )
        below = my_row * n_col + row >= col * n_col + my_col
        parts[row] += product * jnp.where(below & (live[0, 0, k] == 1), 1.0, 0.0)


def body(vectors, tiles, tile_rows, tile_cols, tile_live):
    nvec, seg = vectors.shape
    n_row = lax.axis_size("row")
    n_col = lax.axis_size("col")
    pairs = n_row // 2
    sides = [(i, i ^ 1) for i in range(n_row)]
    order = list(range(pairs))[::-1]
    spots = jnp.array([order.index(p) for p in range(pairs)], jnp.int32)
    params = pltpu.CompilerParams(vmem_limit_bytes=4 << 20)

    columns = sorted(range(n_col), key=lambda c: seat(c, n_col))
    near = [[(2 * p + side) * n_col + c for c in columns for side in range(2)] for p in range(pairs)]
    row_sets = exchange(jnp.broadcast_to(vectors[None], (2 * n_col, nvec, seg)), ("row", "col"), near)
    blocks = tiles.reshape(-1, 128, 128)
    count = blocks.shape[0]
    slots = (tile_rows, tile_cols, tile_live)
    staged = pl.pallas_call(
        stage_kernel,
        out_shape=jax.ShapeDtypeStruct((count + 1, 128, 128), blocks.dtype),
        in_specs=[VMEM] * 3 + [pl.BlockSpec(memory_space=pl.ANY)],
        out_specs=pl.BlockSpec(memory_space=pl.ANY),
        scratch_shapes=[
            pltpu.VMEM((1, 128, 128), blocks.dtype),
            pltpu.VMEM((128, 128), jnp.float32),
            pltpu.SemaphoreType.DMA((9,)),
        ],
        cost_estimate=pl.CostEstimate(flops=0, bytes_accessed=4 * blocks.size, transcendentals=0),
        name="stage",
    )(*slots, blocks)
    other = lax.ppermute(staged, "row", sides)

    own_sums = pl.pallas_call(
        lambda *refs: own_kernel(n_col, *refs),
        out_shape=jax.ShapeDtypeStruct((pairs, nvec, seg), jnp.float32),
        in_specs=[SMEM] * 3 + [VMEM] * 2,
        out_specs=VMEM,
        compiler_params=params,
        cost_estimate=pl.CostEstimate(flops=10**11, bytes_accessed=2 * blocks.size, transcendentals=0),
        name="own",
    )(*slots, row_sets, staged)
    outgoing = pl.pallas_call(
        lambda *refs: pair_kernel(n_col, order, *refs),
        out_shape=jax.ShapeDtypeStruct((pairs, 2, nvec, seg), jnp.bfloat16),
        in_specs=[VMEM] * 3,
        out_specs=VMEM,
        scratch_shapes=[
            pltpu.VMEM((pairs, nvec, seg), jnp.float32),
            pltpu.VMEM((16, 128), jnp.int32),
            pltpu.SMEM((16, 128), jnp.int32),
            pltpu.SemaphoreType.DMA,
        ],
        compiler_params=params,
        name="pair",
    )(row_sets, other, own_sums)
    far = [[2 * p + side for p in order] for side in range(2)]
    arrived = exchange(outgoing, "row", far)
    direct, mirrored = pl.pallas_call(
        lambda *refs: direct_kernel(n_col, order, *refs),
        out_shape=[
            jax.ShapeDtypeStruct((n_col, nvec, seg), jnp.float32),
            jax.ShapeDtypeStruct((nvec, seg), jnp.float32),
        ],
        in_specs=[SMEM] * 4 + [VMEM] * 3,
        out_specs=[VMEM, VMEM],
        compiler_params=params,
        name="direct",
    )(spots, *slots, row_sets, arrived, staged)
    straight = exchange(direct, "col", None)
    return mirrored + jnp.sum(straight, axis=0)


def solution(mesh):
    return jax.shard_map(
        body,
        mesh=mesh,
        in_specs=(
            P(None, ("row", "col")),
            P("row", "col", None, None, None),
            P("row", "col", None),
            P("row", "col", None),
            P("row", "col", None),
        ),
        out_specs=P(None, ("row", "col")),
        check_vma=False,
    )
```

```python
import jax
import jax.numpy as jnp
from jax import lax
from jax.experimental import pallas as pl
from jax.experimental.pallas import tpu as pltpu
from jax.sharding import PartitionSpec as P

SMEM = pl.BlockSpec(memory_space=pltpu.SMEM)
VMEM = pl.BlockSpec(memory_space=pltpu.VMEM)


def exchange(parts, axes, groups):
    return lax.all_to_all(parts, axes, 0, 0, tiled=True, axis_index_groups=groups)


def seat(col, n_col):
    half = n_col // 4
    y = col >> 1
    return ((y & (half - 1)) << 2) | ((y >> (half.bit_length() - 1)) << 1) | (col & 1)


def stage_kernel(lists, tiles, out, notes, sem):
    count = tiles.shape[0]
    notes[...] = jnp.zeros_like(notes)
    notes[pl.ds(0, lists.shape[0]), pl.ds(0, count)] = lists[...].astype(jnp.float32)
    out[count] = notes[...].astype(out.dtype)
    copy = pltpu.make_async_copy(tiles, out.at[pl.ds(0, count)], sem)
    copy.start()
    copy.wait()


def add_mirror(n_col, who, slot, count, row_sets, tiles, sums):
    my_row, my_col = lax.axis_index("row"), lax.axis_index("col")
    pair, side = my_row >> 1, my_row & 1
    for k in range(count):
        row, col, live = slot(k)
        product = jnp.dot(row_sets[2 * n_col - 1 - ((seat(row, n_col) << 1) | who)], tiles[k], preferred_element_type=jnp.float32)
        below = (2 * pair + who) * n_col + row > col * n_col + my_col
        weight = jnp.where(below & ((col & 1) == side) & (live == 1), 1.0, 0.0)
        sums[col >> 1] += product * weight


def own_kernel(n_col, lists, row_sets, staged, sums):
    sums[...] = jnp.zeros_like(sums)
    slot = lambda k: (lists[0, k], lists[1, k], lists[2, k])
    add_mirror(n_col, lax.axis_index("row") & 1, slot, lists.shape[1], row_sets, staged, sums)


def pair_kernel(n_col, order, row_sets, other, own_sums, parts, sums, page, notes, sem):
    count = other.shape[0] - 1
    page[...] = other[count, pl.ds(0, page.shape[0]), :].astype(jnp.float32).astype(jnp.int32)
    copy = pltpu.make_async_copy(page, notes, sem)
    copy.start()
    my_row, my_col = lax.axis_index("row"), lax.axis_index("col")
    pair = my_row >> 1
    sums[...] = own_sums[...]
    copy.wait()
    slot = lambda k: (notes[0, k], notes[1, k], notes[2, k])
    add_mirror(n_col, 1 - (my_row & 1), slot, count, row_sets, other, sums)
    base = 2 * n_col - 1 - (seat(my_col, n_col) << 1)
    first, second = row_sets[base], row_sets[base - 1]
    for at, p in enumerate(order):
        high = sums[p].astype(jnp.bfloat16)
        low = (sums[p] - high.astype(jnp.float32)).astype(jnp.bfloat16)
        parts[at, 0] = jnp.where(p > pair, first, high)
        parts[at, 1] = jnp.where(p > pair, second, low)


def direct_kernel(n_col, order, spots, lists, row_sets, arrived, staged, parts, mirrored):
    my_row, my_col = lax.axis_index("row"), lax.axis_index("col")
    pair = my_row >> 1
    total = jnp.zeros(mirrored.shape, jnp.float32)
    for at, p in enumerate(order):
        both = arrived[at, 0].astype(jnp.float32) + arrived[at, 1].astype(jnp.float32)
        total += jnp.where(p >= pair, both, 0.0)
    mirrored[...] = total
    parts[...] = jnp.zeros_like(parts)
    base = 2 * n_col - 1 - (seat(my_col, n_col) << 1)
    for k in range(lists.shape[1]):
        row, col = lists[0, k], lists[1, k]
        here = row_sets[base - (col & 1)]
        values = jnp.where((col >> 1) == pair, here, arrived[spots[col >> 1], col & 1])
        product = lax.dot_general(
            values, staged[k], (((1,), (1,)), ((), ())), preferred_element_type=jnp.float32
        )
        below = my_row * n_col + row >= col * n_col + my_col
        parts[n_col - 1 - row] += product * jnp.where(below & (lists[2, k] == 1), 1.0, 0.0)


def body(vectors, tiles, tile_rows, tile_cols, tile_live):
    nvec, seg = vectors.shape
    n_row = lax.axis_size("row")
    n_col = lax.axis_size("col")
    pairs = n_row // 2
    sides = [(i, i ^ 1) for i in range(n_row)]
    order = list(range(pairs))[::-1]
    spots = jnp.array([order.index(p) for p in range(pairs)], jnp.int32)
    params = pltpu.CompilerParams(vmem_limit_bytes=4 << 20)

    columns = sorted(range(n_col), key=lambda c: seat(c, n_col))
    near = [[(2 * p + side) * n_col + c for c in columns[::-1] for side in (1, 0)] for p in range(pairs)]
    row_sets = exchange(jnp.broadcast_to(vectors[None], (2 * n_col, nvec, seg)), ("row", "col"), near)
    blocks = tiles.reshape(-1, 128, 128)
    count = blocks.shape[0]
    lists = jnp.stack([slots.reshape(-1) for slots in (tile_rows, tile_cols, tile_live)])
    staged = pl.pallas_call(
        stage_kernel,
        out_shape=jax.ShapeDtypeStruct((count + 1, 128, 128), blocks.dtype),
        in_specs=[VMEM] * 2,
        out_specs=VMEM,
        scratch_shapes=[pltpu.VMEM((128, 128), jnp.float32), pltpu.SemaphoreType.DMA],
        compiler_params=params,
        cost_estimate=pl.CostEstimate(flops=0, bytes_accessed=4 * blocks.size, transcendentals=0),
        name="stage",
    )(lists, blocks)
    other = lax.ppermute(staged, "row", sides)

    own_sums = pl.pallas_call(
        lambda *refs: own_kernel(n_col, *refs),
        out_shape=jax.ShapeDtypeStruct((pairs, nvec, seg), jnp.float32),
        in_specs=[SMEM] + [VMEM] * 2,
        out_specs=VMEM,
        compiler_params=params,
        cost_estimate=pl.CostEstimate(flops=10**11, bytes_accessed=2 * blocks.size, transcendentals=0),
        name="own",
    )(lists, row_sets, staged)
    outgoing = pl.pallas_call(
        lambda *refs: pair_kernel(n_col, order, *refs),
        out_shape=jax.ShapeDtypeStruct((pairs, 2, nvec, seg), jnp.bfloat16),
        in_specs=[VMEM] * 3,
        out_specs=VMEM,
        scratch_shapes=[
            pltpu.VMEM((pairs, nvec, seg), jnp.float32),
            pltpu.VMEM((16, 128), jnp.int32),
            pltpu.SMEM((16, 128), jnp.int32),
            pltpu.SemaphoreType.DMA,
        ],
        compiler_params=params,
        name="pair",
    )(row_sets, other, own_sums)
    far = [[2 * p + side for p in order] for side in range(2)]
    arrived = exchange(outgoing, "row", far)
    direct, mirrored = pl.pallas_call(
        lambda *refs: direct_kernel(n_col, order, *refs),
        out_shape=[
            jax.ShapeDtypeStruct((n_col, nvec, seg), jnp.float32),
            jax.ShapeDtypeStruct((nvec, seg), jnp.float32),
        ],
        in_specs=[SMEM] * 2 + [VMEM] * 3,
        out_specs=[VMEM, VMEM],
        compiler_params=params,
        name="direct",
    )(spots, lists, row_sets, arrived, staged)
    straight = exchange(direct, "col", [list(range(n_col))[::-1]])
    return mirrored + jnp.sum(straight, axis=0)


def solution(mesh):
    return jax.shard_map(
        body,
        mesh=mesh,
        in_specs=(
            P(None, ("row", "col")),
            P("row", "col", None, None, None),
            P("row", "col", None),
            P("row", "col", None),
            P("row", "col", None),
        ),
        out_specs=P(None, ("row", "col")),
        check_vma=False,
    )
```

```python
import jax
import jax.numpy as jnp
from jax import lax
from jax.experimental import pallas as pl
from jax.experimental.pallas import tpu as pltpu
from jax.sharding import PartitionSpec as P

SMEM = pl.BlockSpec(memory_space=pltpu.SMEM)
VMEM = pl.BlockSpec(memory_space=pltpu.VMEM)


def exchange(parts, axes, groups):
    return lax.all_to_all(parts, axes, 0, 0, tiled=True, axis_index_groups=groups)


def stage_kernel(lists, tiles, out, notes, sem):
    count = tiles.shape[0]
    notes[...] = jnp.zeros_like(notes)
    notes[pl.ds(0, lists.shape[0]), pl.ds(0, count)] = lists[...].astype(jnp.float32)
    out[count] = notes[...].astype(out.dtype)
    copy = pltpu.make_async_copy(tiles, out.at[pl.ds(0, count)], sem)
    copy.start()
    copy.wait()


def add_mirror(n_col, who, slot, count, row_sets, tiles, sums):
    my_row, my_col = lax.axis_index("row"), lax.axis_index("col")
    pair, side = my_row >> 1, my_row & 1
    for k in range(count):
        row, col, live = slot(k)
        product = jnp.dot(row_sets[2 * n_col - 1 - ((row << 1) | who)], tiles[k], preferred_element_type=jnp.float32)
        below = (2 * pair + who) * n_col + row > col * n_col + my_col
        weight = jnp.where(below & ((col & 1) == side) & (live == 1), 1.0, 0.0)
        sums[col >> 1] += product * weight


def own_kernel(n_col, lists, row_sets, staged, sums):
    sums[...] = jnp.zeros_like(sums)
    slot = lambda k: (lists[0, k], lists[1, k], lists[2, k])
    add_mirror(n_col, lax.axis_index("row") & 1, slot, lists.shape[1], row_sets, staged, sums)


def pair_kernel(n_col, order, row_sets, other, own_sums, parts, sums, page, notes, sem):
    count = other.shape[0] - 1
    page[...] = other[count, pl.ds(0, page.shape[0]), :].astype(jnp.float32).astype(jnp.int32)
    copy = pltpu.make_async_copy(page, notes, sem)
    copy.start()
    my_row, my_col = lax.axis_index("row"), lax.axis_index("col")
    pair = my_row >> 1
    sums[...] = own_sums[...]
    copy.wait()
    slot = lambda k: (notes[0, k], notes[1, k], notes[2, k])
    add_mirror(n_col, 1 - (my_row & 1), slot, count, row_sets, other, sums)
    base = 2 * n_col - 1 - (my_col << 1)
    first, second = row_sets[base], row_sets[base - 1]
    for at, p in enumerate(order):
        high = sums[p].astype(jnp.bfloat16)
        low = (sums[p] - high.astype(jnp.float32)).astype(jnp.bfloat16)
        parts[at, 0] = jnp.where(p > pair, first, high)
        parts[at, 1] = jnp.where(p > pair, second, low)


def direct_kernel(n_col, order, spots, lists, row_sets, arrived, staged, parts, mirrored):
    my_row, my_col = lax.axis_index("row"), lax.axis_index("col")
    pair = my_row >> 1
    total = jnp.zeros(mirrored.shape, jnp.float32)
    for at, p in enumerate(order):
        both = arrived[at, 0].astype(jnp.float32) + arrived[at, 1].astype(jnp.float32)
        total += jnp.where(p >= pair, both, 0.0)
    mirrored[...] = total
    parts[...] = jnp.zeros_like(parts)
    base = 2 * n_col - 1 - (my_col << 1)
    for k in range(lists.shape[1]):
        row, col = lists[0, k], lists[1, k]
        here = row_sets[base - (col & 1)]
        values = jnp.where((col >> 1) == pair, here, arrived[spots[col >> 1], col & 1])
        product = lax.dot_general(
            values, staged[k], (((1,), (1,)), ((), ())), preferred_element_type=jnp.float32
        )
        below = my_row * n_col + row >= col * n_col + my_col
        parts[n_col - 1 - row] += product * jnp.where(below & (lists[2, k] == 1), 1.0, 0.0)


def body(vectors, tiles, tile_rows, tile_cols, tile_live):
    nvec, seg = vectors.shape
    n_row = lax.axis_size("row")
    n_col = lax.axis_size("col")
    pairs = n_row // 2
    sides = [(i, i ^ 1) for i in range(n_row)]
    order = list(range(pairs))[::-1]
    spots = jnp.array([order.index(p) for p in range(pairs)], jnp.int32)
    params = pltpu.CompilerParams(vmem_limit_bytes=4 << 20)

    columns = list(range(n_col))
    near = [[(2 * p + side) * n_col + c for c in columns[::-1] for side in (1, 0)] for p in range(pairs)]
    row_sets = exchange(jnp.broadcast_to(vectors[None], (2 * n_col, nvec, seg)), ("row", "col"), near)
    blocks = tiles.reshape(-1, 128, 128)
    count = blocks.shape[0]
    lists = jnp.stack([slots.reshape(-1) for slots in (tile_rows, tile_cols, tile_live)])
    staged = pl.pallas_call(
        stage_kernel,
        out_shape=jax.ShapeDtypeStruct((count + 1, 128, 128), blocks.dtype),
        in_specs=[VMEM] * 2,
        out_specs=VMEM,
        scratch_shapes=[pltpu.VMEM((128, 128), jnp.float32), pltpu.SemaphoreType.DMA],
        compiler_params=params,
        cost_estimate=pl.CostEstimate(flops=0, bytes_accessed=4 * blocks.size, transcendentals=0),
        name="stage",
    )(lists, blocks)
    other = lax.ppermute(staged, "row", sides)

    own_sums = pl.pallas_call(
        lambda *refs: own_kernel(n_col, *refs),
        out_shape=jax.ShapeDtypeStruct((pairs, nvec, seg), jnp.float32),
        in_specs=[SMEM] + [VMEM] * 2,
        out_specs=VMEM,
        compiler_params=params,
        cost_estimate=pl.CostEstimate(flops=10**11, bytes_accessed=2 * blocks.size, transcendentals=0),
        name="own",
    )(lists, row_sets, staged)
    outgoing = pl.pallas_call(
        lambda *refs: pair_kernel(n_col, order, *refs),
        out_shape=jax.ShapeDtypeStruct((pairs, 2, nvec, seg), jnp.bfloat16),
        in_specs=[VMEM] * 3,
        out_specs=VMEM,
        scratch_shapes=[
            pltpu.VMEM((pairs, nvec, seg), jnp.float32),
            pltpu.VMEM((16, 128), jnp.int32),
            pltpu.SMEM((16, 128), jnp.int32),
            pltpu.SemaphoreType.DMA,
        ],
        compiler_params=params,
        name="pair",
    )(row_sets, other, own_sums)
    far = [[2 * p + side for p in order] for side in range(2)]
    arrived = exchange(outgoing, "row", far)
    direct, mirrored = pl.pallas_call(
        lambda *refs: direct_kernel(n_col, order, *refs),
        out_shape=[
            jax.ShapeDtypeStruct((n_col, nvec, seg), jnp.float32),
            jax.ShapeDtypeStruct((nvec, seg), jnp.float32),
        ],
        in_specs=[SMEM] * 2 + [VMEM] * 3,
        out_specs=[VMEM, VMEM],
        compiler_params=params,
        name="direct",
    )(spots, lists, row_sets, arrived, staged)
    straight = exchange(direct, "col", [columns[::-1]])
    return mirrored + jnp.sum(straight, axis=0)


def solution(mesh):
    return jax.shard_map(
        body,
        mesh=mesh,
        in_specs=(
            P(None, ("row", "col")),
            P("row", "col", None, None, None),
            P("row", "col", None),
            P("row", "col", None),
            P("row", "col", None),
        ),
        out_specs=P(None, ("row", "col")),
        check_vma=False,
    )
```
